512 devices in a mesh: dp: 32 (over z, x_hi), vocab: 8 (over y, core), ends: 2 (over x_lo).
Axes of the slice: x: 4 (x_hi: 2, x_lo: 2; x = x_hi * 2 + x_lo), y: 4, z: 16, core: 2. Of those that a mesh axis runs over, the one named last changes fastest.
Arguments:
- hidden: bfloat16 [16384, 4608], P('dp', 'ends'), may hold values from -6 to 6
- cotangent: bfloat16 [16384, 4608], P('dp', 'ends'), may hold values from -0.09375 to 0.09375
- token_ids: int32 [16384], P('dp'), may hold values from 0 to 4095
- target_ids: int32 [16384], P('dp'), may hold values from 0 to 4095
- loss_mask: int32 [16384], P('dp'), may hold values 0 or 1
- embedding: bfloat16 [4096, 4608], P('vocab', 'ends'), may hold values from -0.375 to 0.375
Outputs:
- weight_grad: bfloat16 [8, 512, 4608], P('vocab', 'dp', 'ends')
The draws below stay inside these ranges and needn't reach their ends.
All inputs are finite; a program needn't handle non-finite values. No bound on the sum of `loss_mask` on one device may be relied on, other than what follows from the above.
Results may differ from the reference program's by a relative error of at most 0.023.
Values may be sent and summed in bfloat16 or wider, within the bound.
A program may use at most 64 MiB of HBM per device.

```python
import math
import jax
import jax.numpy as jnp
import numpy as np
from jax import lax

D = 4608
VOC_DEV = 512
TOK_DEV = 512
TOKENS = 16384
VOCAB = 4096
N_DP = 32


def place_ends(drawn, stream_key, low, largest):
    place = [jax.random.randint(jax.random.fold_in(stream_key, axis), (), 0, length) for axis, length in enumerate(drawn.shape)]
    widest = drawn.shape.index(max(drawn.shape))
    neighbour = place[:widest] + [(place[widest] + 1) % drawn.shape[widest]] + place[widest + 1:]
    return drawn.at[tuple(place)].set(low).at[tuple(neighbour)].set(largest)


def shard_levels(own_key, extent, pieces, low, high):
    loudness = 1.0
    for axis_at, blocks in pieces:
        heights = jax.random.uniform(jax.random.fold_in(jax.random.fold_in(own_key, 6), axis_at), (blocks,), jnp.float32, low / len(pieces), high / len(pieces))
        loudness = loudness * jnp.repeat(jnp.exp(heights), extent[axis_at] // blocks).reshape((-1,) + (1,) * (len(extent) - 1 - axis_at))
    return loudness


def rank_bounds(number_of, lean):
    loads = [(1 << 20) // math.isqrt(rank ** lean) + 1 for rank in range(1, number_of + 1)]
    width = 1 + sum(loads) // (1 << 30)
    return np.cumsum(np.array([max(1, weight // width) for weight in loads]))


def skewed_ids(key, shape, count, skew):
    table = rank_bounds(count, skew)
    pick = jax.random.randint(jax.random.fold_in(key, 1), shape, 0, int(table[count - 1]))
    standing = jnp.searchsorted(jnp.asarray(table, jnp.int32), pick, side="right")
    return jax.random.permutation(jax.random.fold_in(key, 2), count)[standing].astype(jnp.int32)


def scatter_about(rng, shape, spread, limit, split=(), kind=jnp.bfloat16):
    result = jax.random.normal(rng, shape, jnp.float32) * spread
    if len(split) > 0:
        result = shard_levels(rng, shape, split, -0.22, 0.18) * result
    return jnp.clip(result, min=-limit, max=limit).astype(kind)


def setup_inputs(seed: int = 0) -> dict:
    keys = jax.random.split(jax.random.key(seed), 7)
    return {
        "hidden": scatter_about(keys[0], (TOKENS, D), 1.0, 6.0, ((0, 32), (1, 2))),
        "cotangent": scatter_about(keys[1], (TOKENS, D), D ** -0.5, 0.09375, ((0, 32), (1, 2))),
        "token_ids": place_ends(skewed_ids(keys[2], (TOKENS,), VOCAB, 1), jax.random.fold_in(keys[2], 3), 0, VOCAB - 1).astype(jnp.int32),
        "target_ids": place_ends(skewed_ids(keys[3], (TOKENS,), VOCAB, 1), jax.random.fold_in(keys[3], 3), 0, VOCAB - 1).astype(jnp.int32),
        "loss_mask": place_ends((jax.random.randint(keys[4], (TOKENS,), 0, 4) < 3).astype(jnp.int32), jax.random.fold_in(keys[4], 1), 0, 1),
        "embedding": scatter_about(keys[5], (VOCAB, D), (D // 16) ** -0.5, 0.375, ((0, 8), (1, 2))),
    }


SOFTCAP = 30.0

def reference(hidden, cotangent, token_ids, target_ids, loss_mask, embedding):
    columns = jnp.arange(VOCAB, dtype=jnp.int32)
    normalizer = jnp.asarray(math.sqrt(D), jnp.float32).astype(jnp.bfloat16)
    nothing = jnp.zeros((), jnp.bfloat16)
    blocks = (hidden.reshape(N_DP, TOK_DEV, D), cotangent.reshape(N_DP, TOK_DEV, D), token_ids.reshape(N_DP, TOK_DEV), target_ids.reshape(N_DP, TOK_DEV), loss_mask.reshape(N_DP, TOK_DEV))

    def group_step(carry, block):
        states, grads_in, inputs, targets, masked = block
        raw = jnp.dot(states, embedding.T, preferred_element_type=jnp.float32)
        logits = SOFTCAP * jnp.tanh(raw / SOFTCAP)
        shifted = jnp.exp(logits - SOFTCAP)
        total = lax.optimization_barrier(jnp.sum(shifted, axis=1))
        hit = (targets[:, None] == columns[None, :]).astype(jnp.float32)
        weight = masked.astype(jnp.float32)
        coeff = (weight[:, None] * (shifted / total[:, None] - hit) * (1.0 - (logits / SOFTCAP) ** 2)).astype(jnp.bfloat16)
        picks = jnp.where(inputs[:, None] == columns[None, :], normalizer, nothing)
        head = lax.dot_general(coeff, states, (((0,), (0,)), ((), ())), preferred_element_type=jnp.float32)
        embed = lax.dot_general(picks, grads_in, (((0,), (0,)), ((), ())), preferred_element_type=jnp.float32)
        partial_g = lax.optimization_barrier((head + embed).astype(jnp.bfloat16))
        return (carry + partial_g.astype(jnp.float32), None)
    init = jnp.zeros((VOCAB, D), jnp.float32)
    summed, _ = lax.scan(group_step, init, blocks)
    return summed.astype(jnp.bfloat16).reshape(VOCAB // VOC_DEV, VOC_DEV, D)
```

```python
import functools
import math

import jax
import jax.numpy as jnp
from jax import lax
from jax.experimental import pallas as pl
from jax.experimental.pallas import tpu as pltpu
from jax.sharding import PartitionSpec as P

D = 4608
SOFTCAP = 30.0
MESH = pl.DeviceIdType.MESH
F32 = jnp.float32
BF16 = jnp.bfloat16
PART = 16
CHUNK = 2 * PART
SUBS = 4


def dot_nt(a, b):
    return lax.dot_general(a, b, (((1,), (1,)), ((), ())), preferred_element_type=F32)


def dot_nn(a, b):
    return lax.dot_general(a, b, (((1,), (0,)), ((), ())), preferred_element_type=F32)


def rows_of(start, size):
    return pl.ds(pl.multiple_of(start, size), size)


def kernel(
    nz, nv, subs,
    hidden, cotangent, embedding, tokens, targets, mask,
    out,
    hid, cot, emb, raw_out, raw_in, own, tanhs, shifted, tot_out, tot_in, coeff, embed,
    part_out, part_in, *rest,
):
    n_subs = len(subs)
    bufs, sems = rest[: 3 * n_subs], rest[3 * n_subs :]
    send, recv, last = bufs[:n_subs], bufs[n_subs : 2 * n_subs], bufs[2 * n_subs :]
    load, raw_s, raw_r, tot_s, tot_r, ag_s, ag_r, ring_s, ring_r, last_s, last_r, part_s, part_r = sems

    d, v, e = lax.axis_index("dp"), lax.axis_index("vocab"), lax.axis_index("ends")
    z, h = d // 2, d % 2
    steps = nz // 2
    rows, half = own.shape
    width = hid.shape[2]

    def at_z(k, other):
        return (lax.rem(z + k + nz, nz) * 2 + (1 - h if other else h), v, e)

    mate = (d, v, 1 - e)
    cross = (z * 2 + 1 - h, v, e)
    ahead = (1, -1)

    barrier = pltpu.get_barrier_semaphore()
    greet = [mate, cross] + [at_z(k, o) for k in ahead for o in (False, True)]
    greet += [(d, lax.rem(v + o, nv), e) for o in range(1, nv)]
    for who in greet:
        pl.semaphore_signal(barrier, inc=1, device_id=who, device_id_type=MESH)

    quarter = rows // 4
    other_tokens, own_tokens = rows_of((1 - e) * half, half), rows_of(e * half, half)
    loads = [pltpu.make_async_copy(hidden.at[other_tokens], hid.at[1], load.at[0])]
    loads += [
        pltpu.make_async_copy(embedding.at[pl.ds(c * quarter, quarter)], emb.at[pl.ds(c * quarter, quarter)], load.at[1 + c])
        for c in range(4)
    ]
    loads += [
        pltpu.make_async_copy(hidden.at[own_tokens], hid.at[0], load.at[5]),
        pltpu.make_async_copy(cotangent, cot, load.at[6]),
    ]
    for copy in loads:
        copy.start()

    def raw_copy(c):
        block = rows_of(c * quarter, quarter)
        return pltpu.make_async_remote_copy(
            src_ref=raw_out.at[block], dst_ref=raw_in.at[block], send_sem=raw_s.at[c], recv_sem=raw_r.at[c],
            device_id=mate, device_id_type=MESH,
        )

    loads[0].wait()
    for c in range(4):
        loads[1 + c].wait()
        block = pl.ds(c * quarter, quarter)
        raw_out[block] = dot_nt(emb[block], hid[1]).astype(BF16)
        if c == 0:
            pl.semaphore_wait(barrier, len(greet))
        raw_copy(c).start()

    loads[5].wait()

    def own_block(c, _):
        block = rows_of(c * quarter, quarter)
        own[block] = dot_nt(emb[block], hid[0])
        return 0

    lax.fori_loop(0, 4, own_block, 0)

    loads[6].wait()
    normalizer = jnp.asarray(math.sqrt(D), F32).astype(BF16)
    first = v * rows

    def embed_block(c, _):
        block = rows_of(c * quarter, quarter)
        index = lax.broadcasted_iota(jnp.int32, (quarter, 2 * half), 0) + (first + c * quarter)
        picks = jnp.where(tokens[...] == index, normalizer.astype(F32), 0.0).astype(BF16)
        third = width // 3 if width % 384 == 0 else width
        for n in range(0, width, third):
            embed[block, pl.ds(n, third)] = dot_nn(picks, cot[:, pl.ds(n, third)])
        return 0

    lax.fori_loop(0, 4, embed_block, 0)

    def soft_block(c, total):
        block = rows_of(c * quarter, quarter)
        raw_copy(c).wait_recv()
        t = jnp.tanh((own[block] + raw_in[block].astype(F32)) * (1.0 / SOFTCAP))
        s = jnp.exp(t * SOFTCAP - SOFTCAP)
        tanhs[block] = t
        shifted[block] = s
        return total + jnp.sum(s, axis=0, keepdims=True)

    total = lax.fori_loop(0, 4, soft_block, jnp.zeros((1, half), F32))
    tot_out[...] = total

    def tot_copy(o, source):
        return pltpu.make_async_remote_copy(
            src_ref=tot_out, dst_ref=tot_in.at[source], send_sem=tot_s.at[o], recv_sem=tot_r.at[source],
            device_id=(d, lax.rem(v + o, nv), e), device_id_type=MESH,
        )

    for o in range(1, nv):
        tot_copy(o, v).start()
    for o in range(1, nv):
        source = lax.rem(v + o, nv)
        tot_copy(o, source).wait_recv()
        total = total + tot_in[source]
    weight = mask[e].astype(F32)
    target = targets[e]
    inverse = 1.0 / total

    def chunk_at(i):
        s, direction = i // 2, i % 2
        return lax.rem(z + jnp.where(direction == 0, steps - s, steps + s), nz)

    def ag_copy(i):
        block = rows_of(chunk_at(i) * CHUNK, CHUNK)
        return pltpu.make_async_remote_copy(
            src_ref=coeff.at[0, block], dst_ref=coeff.at[1, block], send_sem=ag_s.at[i], recv_sem=ag_r.at[i],
            device_id=mate, device_id_type=MESH,
        )

    def coeff_block(j, _):
        i = jnp.where(j == 0, 0, j + 1)
        start = chunk_at(i) * CHUNK
        block = rows_of(start, CHUNK)
        index = lax.broadcasted_iota(jnp.int32, (CHUNK, half), 0) + (first + start)
        hit = jnp.where(target == index, 1.0, 0.0)
        t = tanhs[block]
        coeff[0, block] = (weight * (shifted[block] * inverse - hit) * (1.0 - t * t)).astype(BF16)
        ag_copy(i).start()
        return 0

    lax.fori_loop(0, nz, coeff_block, 0)

    def partial_sums(chunks, c0, w):
        blocks = [rows_of(c * CHUNK, CHUNK) for c in chunks]
        cols = pl.ds(c0, w)
        got = embed[blocks[0], cols] if len(blocks) == 1 else jnp.concatenate([embed[b, cols] for b in blocks], axis=0)
        for k in (0, 1):
            left = coeff[k, blocks[0]] if len(blocks) == 1 else jnp.concatenate([coeff[k, b] for b in blocks], axis=0)
            got = got + dot_nn(left, hid[k, :, cols])
        return got

    def ring_copy(direction, u, s):
        return pltpu.make_async_remote_copy(
            src_ref=send[u].at[direction, s], dst_ref=recv[u].at[direction, s],
            send_sem=ring_s.at[direction, u, s], recv_sem=ring_r.at[direction, u, s],
            device_id=at_z(ahead[direction], False), device_id_type=MESH,
        )

    def last_copy(direction, u, other):
        target_h = 1 - h if other else h
        return pltpu.make_async_remote_copy(
            src_ref=send[u].at[direction, steps - 1, rows_of(target_h * PART, PART)],
            dst_ref=last[u].at[direction, h],
            send_sem=last_s.at[direction, u, int(other)], recv_sem=last_r.at[direction, u, h],
            device_id=at_z(ahead[direction], other), device_id_type=MESH,
        )

    def last_wait(direction, u, source):
        pltpu.make_async_remote_copy(
            src_ref=send[u].at[direction, steps - 1, pl.ds(0, PART)],
            dst_ref=last[u].at[direction, source],
            send_sem=last_s.at[direction, u, 0], recv_sem=last_r.at[direction, u, source],
            device_id=at_z(ahead[direction], False), device_id_type=MESH,
        ).wait_recv()

    part_copy = pltpu.make_async_remote_copy(
        src_ref=part_out.at[rows_of((1 - h) * PART, PART)], dst_ref=part_in, send_sem=part_s, recv_sem=part_r,
        device_id=cross, device_id_type=MESH,
    )

    ag_copy(0).wait_recv()
    for u, (c0, w) in enumerate(subs):
        send[u][u % 2, 0] = partial_sums([chunk_at(0)], c0, w).astype(BF16)
        ring_copy(u % 2, u, 0).start()

    def ring_step(s, _):
        for i in (0, 1):
            ag_copy(2 * s + i).wait_recv()
        for u, (c0, w) in enumerate(subs):
            local = partial_sums([chunk_at(2 * s), chunk_at(2 * s + 1)], c0, w)
            for direction in (0, 1):
                mine = local[direction * CHUNK : (direction + 1) * CHUNK]
                if direction == u % 2:
                    ring_copy(direction, u, s - 1).wait_recv()
                    send[u][direction, s] = (mine + recv[u][direction, s - 1].astype(F32)).astype(BF16)
                else:
                    @pl.when(s == 1)
                    def _():
                        send[u][direction, s] = mine.astype(BF16)

                    @pl.when(s > 1)
                    def _():
                        ring_copy(direction, u, s - 1).wait_recv()
                        send[u][direction, s] = (mine + recv[u][direction, s - 1].astype(F32)).astype(BF16)

                @pl.when(s < steps - 1)
                def _():
                    ring_copy(direction, u, s).start()

                @pl.when(s == steps - 1)
                def _():
                    last_copy(direction, u, True).start()
                    last_copy(direction, u, False).start()
        return 0

    lax.fori_loop(1, steps, ring_step, 0)

    ag_copy(2 * steps).wait_recv()
    mine = []
    for u, (c0, w) in enumerate(subs):
        local = partial_sums([z], c0, w)
        part_out[:, pl.ds(c0, w)] = local.astype(BF16)
    part_copy.start()
    part_copy.wait_recv()
    for u, (c0, w) in enumerate(subs):
        for direction in (0, 1):
            for source in (0, 1):
                last_wait(direction, u, source)
        cols = pl.ds(c0, w)
        got = part_out[rows_of(h * PART, PART), cols].astype(F32) + part_in[:, cols].astype(F32)
        for direction in (0, 1):
            for source in (0, 1):
                got = got + last[u][direction, source].astype(F32)
        out[:, cols] = got.astype(BF16)

    for c in range(4):
        raw_copy(c).wait_send()
    for o in range(1, nv):
        tot_copy(o, v).wait_send()
    ag_copy(0).wait_send()

    def ag_done(i, _):
        ag_copy(i).wait_send()
        return 0

    lax.fori_loop(2, 2 * steps + 1, ag_done, 0)
    part_copy.wait_send()
    for u in range(n_subs):
        for direction in (0, 1):
            def ring_done(s, _):
                ring_copy(direction, u, s).wait_send()
                return 0

            lax.fori_loop(0 if direction == u % 2 else 1, steps - 1, ring_done, 0)
            for other in (True, False):
                last_copy(direction, u, other).wait_send()


def solution(mesh):
    nz, nv = mesh.shape["dp"] // 2, mesh.shape["vocab"]

    def shards(hidden, cotangent, token_ids, target_ids, loss_mask, embedding):
        tokens, width = hidden.shape
        rows = embedding.shape[0]
        half = tokens // 2
        steps = nz // 2
        ends = [width // 128 * i // SUBS * 128 for i in range(SUBS + 1)]
        subs = tuple((lo, hi - lo) for lo, hi in zip(ends, ends[1:]))
        any_space = pl.BlockSpec(memory_space=pl.ANY)
        in_vmem = pl.BlockSpec(memory_space=pltpu.VMEM)
        dma = pltpu.SemaphoreType.DMA
        scratch = [
            pltpu.VMEM((2, half, width), BF16),
            pltpu.VMEM((tokens, width), BF16),
            pltpu.VMEM((rows, width), BF16),
            pltpu.VMEM((rows, half), BF16),
            pltpu.VMEM((rows, half), BF16),
            pltpu.VMEM((rows, half), F32),
            pltpu.VMEM((rows, half), F32),
            pltpu.VMEM((rows, half), F32),
            pltpu.VMEM((1, half), F32),
            pltpu.VMEM((nv, 1, half), F32),
            pltpu.VMEM((2, rows, half), BF16),
            pltpu.VMEM((rows, width), F32),
            pltpu.VMEM((CHUNK, width), BF16),
            pltpu.VMEM((PART, width), BF16),
        ]
        scratch += [pltpu.VMEM((2, steps, CHUNK, w), BF16) for _, w in subs]
        scratch += [pltpu.VMEM((2, steps, CHUNK, w), BF16) for _, w in subs]
        scratch += [pltpu.VMEM((2, 2, PART, w), BF16) for _, w in subs]
        scratch += [
            dma((7,)), dma((4,)), dma((4,)), dma((nv,)), dma((nv,)),
            dma((2 * steps + 1,)), dma((2 * steps + 1,)),
            dma((2, SUBS, steps)), dma((2, SUBS, steps)), dma((2, SUBS, 2)), dma((2, SUBS, 2)), dma, dma,
        ]
        got = pl.pallas_call(
            functools.partial(kernel, nz, nv, subs),
            out_shape=jax.ShapeDtypeStruct((rows // (2 * nz), width), BF16),
            in_specs=[any_space] * 3 + [in_vmem] * 3,
            out_specs=in_vmem,
            scratch_shapes=scratch,
            compiler_params=pltpu.CompilerParams(
                collective_id=0, has_side_effects=True, vmem_limit_bytes=48 * 2**20
            ),
        )(
            hidden, cotangent, embedding,
            token_ids.reshape(1, tokens), target_ids.reshape(2, 1, half), loss_mask.reshape(2, 1, half),
        )
        return got[None]

    return jax.shard_map(
        shards,
        mesh=mesh,
        in_specs=(P("dp", "ends"), P("dp", "ends"), P("dp"), P("dp"), P("dp"), P("vocab", "ends")),
        out_specs=P("vocab", "dp", "ends"),
        check_vma=False,
    )
```

```python
import functools
import math

import jax
import jax.numpy as jnp
from jax import lax
from jax.experimental import pallas as pl
from jax.experimental.pallas import tpu as pltpu
from jax.sharding import PartitionSpec as P

D = 4608
SOFTCAP = 30.0
MESH = pl.DeviceIdType.MESH
F32 = jnp.float32
BF16 = jnp.bfloat16
VMEM_LIMIT = 62 * 2**20
PART = 16
CHUNK = 2 * PART
RAW = 2
BLOCKS = ((5, False), (4, False), (5, True), (4, True))


def dot_nt(a, b):
    return lax.dot_general(a, b, (((1,), (1,)), ((), ())), preferred_element_type=F32)


def dot_nn(a, b):
    return lax.dot_general(a, b, (((1,), (0,)), ((), ())), preferred_element_type=F32)


def rows_of(start, size):
    return pl.ds(pl.multiple_of(start, size), size)


def kernel(
    nz, nv, subs, col_x,
    hidden, cotangent, embedding, tokens_in, targets_in, mask_in,
    out,
    tokens, targets, mask, hid, cot, emb, raw_out, raw_in, own, tanhs, shifted, tot_out, tot_in, coeff, sums,
    part_out, part_in, cross_out, cross_in, *rest,
):
    n_subs = len(subs)
    send, recv, sems = rest[:n_subs], rest[n_subs : 2 * n_subs], rest[2 * n_subs :]
    (load, raw_s, raw_r, tot_s, tot_r, ag_s, ag_r, ring_s, ring_r, diag_s, diag_r,
     cross_s, cross_r, part_s, part_r) = sems

    d, v, e = lax.axis_index("dp"), lax.axis_index("vocab"), lax.axis_index("ends")
    z, h = d // 2, d % 2
    steps = nz // 2
    rows, half = own.shape
    width = hid.shape[2]

    def at_z(k, other):
        return (lax.rem(z + k + nz, nz) * 2 + (1 - h if other else h), v, e)

    mate = (d, v, 1 - e)
    across = (z * 2 + 1 - h, v, e)
    ahead = (1, -1)

    quarter = rows // RAW
    other_tokens, own_tokens = rows_of((1 - e) * half, half), rows_of(e * half, half)
    pairs = [(hidden.at[other_tokens], hid.at[1])]
    pairs += [(embedding.at[pl.ds(c * quarter, quarter)], emb.at[pl.ds(c * quarter, quarter)]) for c in range(RAW)]
    pairs += [(hidden.at[own_tokens], hid.at[0]), (tokens_in, tokens), (cotangent, cot), (targets_in, targets), (mask_in, mask)]
    loads = [pltpu.make_async_copy(a, b, load.at[i]) for i, (a, b) in enumerate(pairs)]
    for copy in loads[: RAW + 1]:
        copy.start()

    barrier = pltpu.get_barrier_semaphore()
    greet = [mate, across] + [at_z(k, o) for k in ahead for o in (False, True)]
    greet += [(d, lax.rem(v + o, nv), e) for o in range(1, nv)]
    for who in greet:
        pl.semaphore_signal(barrier, inc=1, device_id=who, device_id_type=MESH)

    def raw_copy(c):
        block = rows_of(c * quarter, quarter)
        return pltpu.make_async_remote_copy(
            src_ref=raw_out.at[block], dst_ref=raw_in.at[block], send_sem=raw_s.at[c], recv_sem=raw_r.at[c],
            device_id=mate, device_id_type=MESH,
        )

    loads[0].wait()
    for c in range(RAW):
        loads[1 + c].wait()
        if c == 0:
            for copy in loads[RAW + 1 :]:
                copy.start()
        block = pl.ds(c * quarter, quarter)
        raw_out[block] = dot_nt(emb[block], hid[1]).astype(BF16)
        if c == 0:
            pl.semaphore_wait(barrier, len(greet))
        raw_copy(c).start()

    loads[RAW + 1].wait()
    for c in range(RAW):
        block = pl.ds(c * quarter, quarter)
        own[block] = dot_nt(emb[block], hid[0])

    for copy in loads[RAW + 2 :]:
        copy.wait()
    normalizer = jnp.asarray(math.sqrt(D), F32).astype(BF16)
    first = v * rows
    fourth = rows // 4

    def embed_block(c, _):
        block = rows_of(c * fourth, fourth)
        index = lax.broadcasted_iota(jnp.int32, (fourth, 2 * half), 0) + (first + c * fourth)
        picks = jnp.where(tokens[...] == index, normalizer.astype(F32), 0.0).astype(BF16)
        third = width // 3 if width % 384 == 0 else width
        for n in range(0, width, third):
            sums[block, pl.ds(n, third)] = dot_nn(picks, cot[:, pl.ds(n, third)])
        return 0

    lax.fori_loop(0, 4, embed_block, 0)

    def soft_block(c, total):
        block = rows_of(c * quarter, quarter)
        raw_copy(c).wait_recv()
        t = jnp.tanh((own[block] + raw_in[block].astype(F32)) * (1.0 / SOFTCAP))
        s = jnp.exp(t * SOFTCAP - SOFTCAP)
        tanhs[block] = t
        shifted[block] = s
        return total + jnp.sum(s, axis=0, keepdims=True)

    total = lax.fori_loop(0, RAW, soft_block, jnp.zeros((1, half), F32))
    tot_out[...] = total

    def tot_copy(o, source):
        return pltpu.make_async_remote_copy(
            src_ref=tot_out, dst_ref=tot_in.at[source], send_sem=tot_s.at[o], recv_sem=tot_r.at[source],
            device_id=(d, lax.rem(v + o, nv), e), device_id_type=MESH,
        )

    for o in range(1, nv):
        tot_copy(o, v).start()
    for o in range(1, nv):
        source = lax.rem(v + o, nv)
        tot_copy(o, source).wait_recv()
        total = total + tot_in[source]
    weight = mask[e].astype(F32)
    target = targets[e]
    inverse = 1.0 / total

    def chunk_at(i):
        s, direction = i // 2, i % 2
        return lax.rem(z + jnp.where(direction == 0, steps - s, steps + s), nz)

    def ag_copy(i):
        block = rows_of(chunk_at(i) * CHUNK, CHUNK)
        return pltpu.make_async_remote_copy(
            src_ref=coeff.at[0, block], dst_ref=coeff.at[1, block], send_sem=ag_s.at[i], recv_sem=ag_r.at[i],
            device_id=mate, device_id_type=MESH,
        )

    def coeff_block(j, _):
        i = jnp.where(j == 0, 0, j + 1)
        start = chunk_at(i) * CHUNK
        block = rows_of(start, CHUNK)
        index = lax.broadcasted_iota(jnp.int32, (CHUNK, half), 0) + (first + start)
        hit = jnp.where(target == index, 1.0, 0.0)
        t = tanhs[block]
        coeff[0, block] = (weight * (shifted[block] * inverse - hit) * (1.0 - t * t)).astype(BF16)
        ag_copy(i).start()
        return 0

    lax.fori_loop(0, nz, coeff_block, 0)

    def complete(chunks, c0, w):
        blocks = [rows_of(c * CHUNK, CHUNK) for c in chunks]
        cols = pl.ds(c0, w)
        got = 0.0
        for k in (0, 1):
            left = coeff[k, blocks[0]] if len(blocks) == 1 else jnp.concatenate([coeff[k, b] for b in blocks], axis=0)
            got = got + dot_nn(left, hid[k, :, cols])
        for i, b in enumerate(blocks):
            sums[b, cols] = sums[b, cols] + got[i * CHUNK : (i + 1) * CHUNK]

    straight_rows, other_rows = rows_of(h * PART, PART), rows_of((1 - h) * PART, PART)

    def ring_copy(direction, u, s, kind):
        source, landing = {
            "full": (pl.ds(0, CHUNK), pl.ds(0, CHUNK)),
            "part": (straight_rows, pl.ds(0, PART)),
            "half": (pl.ds(0, PART), pl.ds(0, PART)),
        }[kind]
        return pltpu.make_async_remote_copy(
            src_ref=send[u].at[direction, s, source], dst_ref=recv[u].at[direction, s, landing],
            send_sem=ring_s.at[direction, u, s], recv_sem=ring_r.at[direction, u, s],
            device_id=at_z(ahead[direction], False), device_id_type=MESH,
        )

    def diag_copy(direction, u):
        s = subs[u][2] - 1
        return pltpu.make_async_remote_copy(
            src_ref=send[u].at[direction, s, other_rows], dst_ref=recv[u].at[direction, s, pl.ds(PART, PART)],
            send_sem=diag_s.at[direction, u], recv_sem=diag_r.at[direction, u],
            device_id=at_z(ahead[direction], True), device_id_type=MESH,
        )

    def cross_copy(direction, s):
        return pltpu.make_async_remote_copy(
            src_ref=cross_out.at[direction, s], dst_ref=cross_in.at[direction, s],
            send_sem=cross_s.at[direction, s], recv_sem=cross_r.at[direction, s],
            device_id=across, device_id_type=MESH,
        )

    part_copy = pltpu.make_async_remote_copy(
        src_ref=part_out, dst_ref=part_in, send_sem=part_s, recv_sem=part_r, device_id=across, device_id_type=MESH,
    )
    cols_x = pl.ds(col_x, width - col_x)

    def row_start(direction, s):
        return chunk_at(2 * s + direction) * CHUNK

    def cross_start(s):
        for direction in (0, 1):
            block = rows_of(row_start(direction, s) + (1 - h) * PART, PART)
            cross_out[direction, s] = sums[block, cols_x].astype(BF16)
            cross_copy(direction, s).start()

    def ring(u, s, direction, fixed):
        c0, w, part = subs[u]
        cols = pl.ds(c0, w)
        start = row_start(direction, s)
        if fixed >= part:
            ring_copy(direction, u, s - 1, "part" if fixed == part else "half").wait_recv()
            got = sums[rows_of(start + h * PART, PART), cols]
            got = got + cross_in[direction, s, :, pl.ds(c0 - col_x, w)].astype(F32)
            got = got + recv[u][direction, s - 1, pl.ds(0, PART)].astype(F32)
            if fixed == part:
                diag_copy(direction, u).wait_recv()
                got = got + recv[u][direction, s - 1, pl.ds(PART, PART)].astype(F32)
            send[u][direction, s, pl.ds(0, PART)] = got.astype(BF16)
            ring_copy(direction, u, s, "half").start()
            return
        got = sums[rows_of(start, CHUNK), cols]
        if fixed > begin(u, direction):
            ring_copy(direction, u, s - 1, "full").wait_recv()
            got = got + recv[u][direction, s - 1].astype(F32)
        send[u][direction, s] = got.astype(BF16)
        if fixed == part - 1:
            diag_copy(direction, u).start()
            ring_copy(direction, u, s, "part").start()
        else:
            ring_copy(direction, u, s, "full").start()

    def begin(u, direction):
        return 0 if direction == u % 2 else 1

    def ag_wait(s, ways=(0, 1)):
        for i in ways:
            ag_copy(2 * s + i).wait_recv()

    def pair(s):
        return [chunk_at(2 * s), chunk_at(2 * s + 1)]

    def iteration(s, fixed):
        later = s + 2
        if fixed < steps - 1:
            ag_wait(later, (0,) if fixed == steps - 2 else (0, 1))
        if fixed >= 2:
            for direction in (0, 1):
                cross_copy(direction, s).wait_recv()
        for u, (c0, w, _) in enumerate(subs):
            for direction in (0, 1):
                if fixed > begin(u, direction):
                    ring(u, s, direction, fixed)
            if fixed < steps - 1:
                complete([z] if fixed == steps - 2 else pair(later), c0, w)
        if fixed < steps - 2:
            cross_start(later)
        if fixed == steps - 2:
            part_out[...] = sums[rows_of(z * CHUNK + (1 - h) * PART, PART)].astype(BF16)
            part_copy.start()

    ag_wait(0, (0,))
    for u, (c0, w, _) in enumerate(subs):
        complete([chunk_at(0)], c0, w)
        ring(u, 0, u % 2, 0)
    ag_wait(1)
    for u, (c0, w, _) in enumerate(subs):
        complete(pair(1), c0, w)
        ring(u, 1, 1 - u % 2, 1)
    ag_wait(2)
    for u, (c0, w, _) in enumerate(subs):
        complete(pair(2), c0, w)
    cross_start(2)

    loop = range(3, steps - 2)
    for s in range(1, steps):
        if s not in loop:
            iteration(s, s)
        elif s == loop[0]:
            def looped(i, _):
                iteration(i, 3)
                return 0

            lax.fori_loop(loop[0], loop[-1] + 1, looped, 0)

    part_copy.wait_recv()
    for u, (c0, w, part) in enumerate(subs):
        cols = pl.ds(c0, w)
        got = sums[rows_of(z * CHUNK + h * PART, PART), cols] + part_in[:, cols].astype(F32)
        for direction in (0, 1):
            ring_copy(direction, u, steps - 1, "part" if part == steps else "half").wait_recv()
            got = got + recv[u][direction, steps - 1, pl.ds(0, PART)].astype(F32)
            if part == steps:
                diag_copy(direction, u).wait_recv()
                got = got + recv[u][direction, steps - 1, pl.ds(PART, PART)].astype(F32)
        out[:, cols] = got.astype(BF16)

    for c in range(RAW):
        raw_copy(c).wait_send()
    for o in range(1, nv):
        tot_copy(o, v).wait_send()
    ag_copy(0).wait_send()

    def ag_done(i, _):
        ag_copy(i).wait_send()
        return 0

    lax.fori_loop(2, 2 * steps + 1, ag_done, 0)
    part_copy.wait_send()
    for direction in (0, 1):
        def cross_done(s, _):
            cross_copy(direction, s).wait_send()
            return 0

        lax.fori_loop(2, steps, cross_done, 0)
    for u, (_, _, part) in enumerate(subs):
        for direction in (0, 1):
            def ring_done(kind, s, _):
                ring_copy(direction, u, s, kind).wait_send()
                return 0

            lax.fori_loop(begin(u, direction), part - 1, functools.partial(ring_done, "full"), 0)
            ring_copy(direction, u, part - 1, "part").wait_send()
            diag_copy(direction, u).wait_send()
            lax.fori_loop(part, steps, functools.partial(ring_done, "half"), 0)


def solution(mesh):
    nz, nv = mesh.shape["dp"] // 2, mesh.shape["vocab"]

    def shards(hidden, cotangent, token_ids, target_ids, loss_mask, embedding):
        tokens, width = hidden.shape
        rows = embedding.shape[0]
        half = tokens // 2
        steps = nz // 2
        shares = sum(share for share, _ in BLOCKS)
        subs, c0 = [], 0
        for share, early in BLOCKS:
            w = width // 128 * share // shares * 128
            subs.append((c0, w, 2 if early else steps))
            c0 += w
        col_x = min(lo for lo, _, part in subs if part == 2)
        any_space = pl.BlockSpec(memory_space=pl.ANY)
        dma = pltpu.SemaphoreType.DMA
        n = len(subs)
        scratch = [
            pltpu.VMEM((1, tokens), jnp.int32),
            pltpu.VMEM((2, 1, half), jnp.int32),
            pltpu.VMEM((2, 1, half), jnp.int32),
            pltpu.VMEM((2, half, width), BF16),
            pltpu.VMEM((tokens, width), BF16),
            pltpu.VMEM((rows, width), BF16),
            pltpu.VMEM((rows, half), BF16),
            pltpu.VMEM((rows, half), BF16),
            pltpu.VMEM((rows, half), F32),
            pltpu.VMEM((rows, half), F32),
            pltpu.VMEM((rows, half), F32),
            pltpu.VMEM((1, half), F32),
            pltpu.VMEM((nv, 1, half), F32),
            pltpu.VMEM((2, rows, half), BF16),
            pltpu.VMEM((rows, width), F32),
            pltpu.VMEM((PART, width), BF16),
            pltpu.VMEM((PART, width), BF16),
            pltpu.VMEM((2, steps, PART, width - col_x), BF16),
            pltpu.VMEM((2, steps, PART, width - col_x), BF16),
        ]
        scratch += [pltpu.VMEM((2, steps, CHUNK, w), BF16) for _, w, _ in subs] * 2
        scratch += [
            dma((RAW + 6,)), dma((RAW,)), dma((RAW,)), dma((nv,)), dma((nv,)),
            dma((2 * steps + 1,)), dma((2 * steps + 1,)),
            dma((2, n, steps)), dma((2, n, steps)), dma((2, n)), dma((2, n)),
            dma((2, steps)), dma((2, steps)), dma, dma,
        ]
        got = pl.pallas_call(
            functools.partial(kernel, nz, nv, subs, col_x),
            out_shape=jax.ShapeDtypeStruct((rows // (2 * nz), width), BF16),
            in_specs=[any_space] * 6,
            out_specs=pl.BlockSpec(memory_space=pltpu.VMEM),
            scratch_shapes=scratch,
            compiler_params=pltpu.CompilerParams(
                collective_id=0, has_side_effects=True, vmem_limit_bytes=VMEM_LIMIT
            ),
        )(
            hidden, cotangent, embedding,
            token_ids.reshape(1, tokens), target_ids.reshape(2, 1, half), loss_mask.reshape(2, 1, half),
        )
        return got[None]

    return jax.shard_map(
        shards,
        mesh=mesh,
        in_specs=(P("dp", "ends"), P("dp", "ends"), P("dp"), P("dp"), P("dp"), P("vocab", "ends")),
        out_specs=P("vocab", "dp", "ends"),
        check_vma=False,
    )
```

```python
import functools
import math

import jax
import jax.numpy as jnp
from jax import lax
from jax.experimental import pallas as pl
from jax.experimental.pallas import tpu as pltpu
from jax.sharding import PartitionSpec as P

D = 4608
SOFTCAP = 30.0
MESH = pl.DeviceIdType.MESH
F32 = jnp.float32
BF16 = jnp.bfloat16
VMEM_LIMIT = 62 * 2**20
PART = 16
CHUNK = 2 * PART
RAW = 4
EARLY = 2
BLOCKS = ((5, False), (4, False), (5, True), (4, True))


def dot_nt(a, b):
    return lax.dot_general(a, b, (((1,), (1,)), ((), ())), preferred_element_type=F32)


def dot_nn(a, b):
    return lax.dot_general(a, b, (((1,), (0,)), ((), ())), preferred_element_type=F32)


def rows_of(start, size):
    return pl.ds(pl.multiple_of(start, size), size)


def kernel(
    nz, nv, subs,
    hidden, cotangent, embedding, tokens_in, targets_in, mask_in,
    out,
    tokens, targets, mask, hid, cot, emb, raw_out, raw_in, own, tilt_out, tilt_in, stats, tot_in, hit_in, sums,
    part_out, part_in, cross_out, cross_in, *rest,
):
    n_subs = len(subs)
    send, recv, sems = rest[:n_subs], rest[n_subs : 2 * n_subs], rest[2 * n_subs :]
    (load, raw_s, raw_r, tot_s, tot_r, tilt_s, tilt_r, hit_s, hit_r, ring_s, ring_r, diag_s, diag_r,
     cross_s, cross_r, part_s, part_r) = sems

    d, v, e = lax.axis_index("dp"), lax.axis_index("vocab"), lax.axis_index("ends")
    z, h = d // 2, d % 2
    steps = nz // 2
    rows, half = own.shape
    width = hid.shape[2]

    def at_z(k, other):
        return (lax.rem(z + k + nz, nz) * 2 + (1 - h if other else h), v, e)

    mate = (d, v, 1 - e)
    across = (z * 2 + 1 - h, v, e)
    ahead = (1, -1)

    def peer(o, f):
        return (d, lax.rem(v + o, nv), (e + f) % 2)

    def chunk_at(place):
        s, direction = (place + 1) // 2, (place + 1) % 2
        return lax.rem(z + (steps - s if direction == 0 or place == 0 else steps + s), nz)

    def place_of(direction, s):
        return 0 if s == 0 else 2 * s - 1 + direction

    def ids_at(place, n):
        return lax.broadcasted_iota(jnp.int32, (CHUNK, n), 0) + (v * rows + chunk_at(place) * CHUNK)

    barrier = pltpu.get_barrier_semaphore()
    greet = [mate, across] + [at_z(k, o) for k in ahead for o in (False, True)] + [at_z(2 * k, False) for k in ahead]
    peers = [(o, f) for o in sorted(range(nv), key=lambda o: -min(o, nv - o)) for f in (1, 0) if (o, f) not in ((0, 0), (0, 1))]
    greet += [peer(o, f) for o, f in peers]
    peers.append((0, 1))
    for who in greet:
        pl.semaphore_signal(barrier, inc=1, device_id=who, device_id_type=MESH)

    quarter = rows // RAW
    per = quarter // CHUNK
    other_tokens, own_tokens = rows_of((1 - e) * half, half), rows_of(e * half, half)
    other_load = pltpu.make_async_copy(hidden.at[other_tokens], hid.at[1], load.at[0])
    other_load.start()
    for place in range(rows // CHUNK):
        pltpu.make_async_copy(
            embedding.at[rows_of(chunk_at(place) * CHUNK, CHUNK)], emb.at[pl.ds(place * CHUNK, CHUNK)],
            load.at[1 + place // per],
        ).start()
    pairs = [(hidden.at[own_tokens], hid.at[0]), (targets_in, targets), (mask_in, mask), (tokens_in, tokens), (cotangent, cot)]
    loads = [pltpu.make_async_copy(a, b, load.at[1 + RAW + i]) for i, (a, b) in enumerate(pairs)]

    def raw_copy(c):
        block = pl.ds(c * quarter, quarter)
        return pltpu.make_async_remote_copy(
            src_ref=raw_out.at[block], dst_ref=raw_in.at[block], send_sem=raw_s.at[c], recv_sem=raw_r.at[c],
            device_id=mate, device_id_type=MESH,
        )

    other_load.wait()
    for c in range(RAW):
        block = pl.ds(c * quarter, quarter)
        pltpu.make_async_copy(embedding.at[block], emb.at[block], load.at[1 + c]).wait()
        raw_out[block] = dot_nt(emb[block], hid[1]).astype(BF16)
        if c == 0:
            pl.semaphore_wait(barrier, len(greet))
        raw_copy(c).start()

    for copy in loads:
        copy.start()
    loads[0].wait()
    for c in range(RAW):
        block = pl.ds(c * quarter, quarter)
        own[block] = dot_nt(emb[block], hid[0])
    loads[1].wait()
    loads[2].wait()

    def tilt_copy(c):
        block = pl.ds(c * quarter, quarter)
        return pltpu.make_async_remote_copy(
            src_ref=tilt_out.at[block], dst_ref=tilt_in.at[block], send_sem=tilt_s.at[c], recv_sem=tilt_r.at[c],
            device_id=mate, device_id_type=MESH,
        )

    def summed(x):
        return jnp.sum(x, axis=0, keepdims=True)

    nothing = jnp.zeros((1, half), F32)
    total, at_shifted, at_slope = nothing, nothing, nothing
    for c in range(RAW):
        raw_copy(c).wait_recv()
        for place in range(c * per, (c + 1) * per):
            block = pl.ds(place * CHUNK, CHUNK)
            t = jnp.tanh((own[block] + raw_in[block].astype(F32)) * (1.0 / SOFTCAP))
            s = jnp.exp(t * SOFTCAP - SOFTCAP)
            slope = 1.0 - t * t
            tilt = s * slope
            own[block] = tilt
            tilt_out[block] = tilt.astype(BF16)
            hit = targets[e] == ids_at(place, half)
            total = total + summed(s)
            at_shifted = at_shifted + summed(jnp.where(hit, s, 0.0))
            at_slope = at_slope + summed(jnp.where(hit, slope, 0.0))
        tilt_copy(c).start()
    stats[0], stats[1], stats[2] = total, at_shifted, at_slope

    def tot_copy(o, f, sent):
        source = (lax.rem(v + o, nv) * 2 + (e + f) % 2) if not sent else v * 2 + e
        return pltpu.make_async_remote_copy(
            src_ref=stats.at[0], dst_ref=tot_in.at[source], send_sem=tot_s.at[o, f], recv_sem=tot_r.at[source],
            device_id=peer(o, f), device_id_type=MESH,
        )

    hit_copy = pltpu.make_async_remote_copy(
        src_ref=stats.at[pl.ds(1, 2)], dst_ref=hit_in, send_sem=hit_s, recv_sem=hit_r, device_id=mate, device_id_type=MESH,
    )
    for o, f in peers:
        tot_copy(o, f, True).start()
    hit_copy.start()
    loads[3].wait()
    loads[4].wait()
    normalizer = jnp.asarray(math.sqrt(D), F32).astype(BF16).astype(F32)
    for c in range(RAW):
        block = pl.ds(c * quarter, quarter)
        picks = [jnp.where(tokens[...] == ids_at(c * per + i, 2 * half), normalizer, 0.0).astype(BF16) for i in range(per)]
        picks = jnp.concatenate(picks, axis=0)
        for c0, w, _ in subs:
            sums[block, pl.ds(c0, w)] = dot_nn(picks, cot[:, pl.ds(c0, w)])

    totals = [total, nothing]
    for o, f in peers:
        tot_copy(o, f, False).wait_recv()
        totals[f] = totals[f] + tot_in[lax.rem(v + o, nv) * 2 + (e + f) % 2]
    hit_copy.wait_recv()
    factors, at_target, wanted = [], [], []
    for f, (a, b) in enumerate(((at_shifted, at_slope), (hit_in[0], hit_in[1]))):
        side = (e + f) % 2
        weight = mask[side].astype(F32)
        inverse = 1.0 / totals[f]
        factors.append(weight * inverse)
        at_target.append(weight * (a * inverse - 1.0) * b)
        wanted.append(targets[side])

    come = []

    def complete(places):
        for c in sorted({place // per for place in places}):
            if c not in come:
                tilt_copy(c).wait_recv()
                come.append(c)
        blocks = [pl.ds(place * CHUNK, CHUNK) for place in places]
        left = []
        for f, tilts in enumerate((own, tilt_in)):
            parts = []
            for place, b in zip(places, blocks):
                hit = wanted[f] == ids_at(place, half)
                parts.append(jnp.where(hit, at_target[f], factors[f] * tilts[b].astype(F32)).astype(BF16))
            left.append(parts[0] if len(parts) == 1 else jnp.concatenate(parts, axis=0))
        for c0, w, _ in subs:
            cols = pl.ds(c0, w)
            got = dot_nn(left[0], hid[0, :, cols]) + dot_nn(left[1], hid[1, :, cols])
            for i, b in enumerate(blocks):
                sums[b, cols] = sums[b, cols] + got[i * CHUNK : (i + 1) * CHUNK]

    straight_rows, other_rows = rows_of(h * PART, PART), rows_of((1 - h) * PART, PART)

    def ring_copy(direction, u, s, kind):
        source, landing = {
            "full": (pl.ds(0, CHUNK), pl.ds(0, CHUNK)),
            "part": (straight_rows, pl.ds(0, PART)),
            "half": (pl.ds(0, PART), pl.ds(0, PART)),
        }[kind]
        return pltpu.make_async_remote_copy(
            src_ref=send[u].at[direction, s, source], dst_ref=recv[u].at[direction, s, landing],
            send_sem=ring_s.at[direction, u, s], recv_sem=ring_r.at[direction, u, s],
            device_id=at_z(ahead[direction] * (2 if s == steps - 2 else 1), False), device_id_type=MESH,
        )

    def diag_copy(direction, u):
        s = subs[u][2] - 1
        return pltpu.make_async_remote_copy(
            src_ref=send[u].at[direction, s, other_rows], dst_ref=recv[u].at[direction, s, pl.ds(PART, PART)],
            send_sem=diag_s.at[direction, u], recv_sem=diag_r.at[direction, u],
            device_id=at_z(ahead[direction], True), device_id_type=MESH,
        )

    def cross_cols(s):
        c0 = min(lo for lo, _, part in subs if part <= s)
        return pl.ds(c0, width - c0)

    def cross_copy(direction, s):
        cols = cross_cols(s)
        return pltpu.make_async_remote_copy(
            src_ref=cross_out.at[direction, s, :, cols], dst_ref=cross_in.at[direction, s, :, cols],
            send_sem=cross_s.at[direction, s], recv_sem=cross_r.at[direction, s],
            device_id=across, device_id_type=MESH,
        )

    part_copy = pltpu.make_async_remote_copy(
        src_ref=part_out, dst_ref=part_in, send_sem=part_s, recv_sem=part_r, device_id=across, device_id_type=MESH,
    )
    def row_start(direction, s):
        return place_of(direction, s) * CHUNK

    def cross_start(s):
        cols = cross_cols(s)
        for direction in (0, 1):
            block = rows_of(row_start(direction, s) + (1 - h) * PART, PART)
            cross_out[direction, s, :, cols] = sums[block, cols].astype(BF16)
            cross_copy(direction, s).start()

    def begin(u, direction):
        return 0 if direction == u % 2 else 1

    def ring(u, s, direction):
        c0, w, part = subs[u]
        cols = pl.ds(c0, w)
        start = row_start(direction, s)
        if s >= part:
            got = sums[rows_of(start + h * PART, PART), cols] + cross_in[direction, s, :, cols].astype(F32)
            if begin(u, direction) < s < steps - 1:
                ring_copy(direction, u, s - 1, "part" if s == part else "half").wait_recv()
                got = got + recv[u][direction, s - 1, pl.ds(0, PART)].astype(F32)
                if s == part:
                    diag_copy(direction, u).wait_recv()
                    got = got + recv[u][direction, s - 1, pl.ds(PART, PART)].astype(F32)
            send[u][direction, s, pl.ds(0, PART)] = got.astype(BF16)
            ring_copy(direction, u, s, "half").start()
            return
        got = sums[pl.ds(start, CHUNK), cols]
        if s > begin(u, direction):
            ring_copy(direction, u, s - 1, "full").wait_recv()
            got = got + recv[u][direction, s - 1].astype(F32)
        send[u][direction, s] = got.astype(BF16)
        if s == part - 1:
            diag_copy(direction, u).start()
            ring_copy(direction, u, s, "part").start()
        else:
            ring_copy(direction, u, s, "full").start()

    def pair(s):
        return [place_of(0, s), place_of(1, s)]

    def cross_wait(s):
        for direction in (0, 1):
            cross_copy(direction, s).wait_recv()

    def sent(s):
        for direction in (0, 1):
            if s >= EARLY:
                cross_copy(direction, s).wait_send()
            for u, (_, _, part) in enumerate(subs):
                if s >= begin(u, direction):
                    kind = "full" if s < part - 1 else "part" if s == part - 1 else "half"
                    ring_copy(direction, u, s, kind).wait_send()
                    if kind == "part":
                        diag_copy(direction, u).wait_send()

    complete([0])
    for u in range(n_subs):
        ring(u, 0, u % 2)
    complete(pair(1))
    if EARLY == 1:
        cross_start(1)
    for u, (_, _, part) in enumerate(subs):
        if part > 1:
            ring(u, 1, 1 - u % 2)
    complete(pair(2))
    if EARLY <= 2:
        cross_start(2)
    if EARLY == 1:
        cross_wait(1)
        for u, (_, _, part) in enumerate(subs):
            if part == 1:
                ring(u, 1, 1 - u % 2)
    for s in range(1, steps - 1):
        if s >= EARLY:
            cross_wait(s)
        for u in range(n_subs):
            for direction in (0, 1):
                if s > begin(u, direction):
                    ring(u, s, direction)
        if s < steps - 2:
            complete(pair(s + 2))
            if s + 2 >= EARLY:
                cross_start(s + 2)
        if s == steps - 3:
            complete([2 * steps - 1])
            part_out[...] = sums[rows_of((2 * steps - 1) * CHUNK + (1 - h) * PART, PART)].astype(BF16)
            part_copy.start()
        if s == 1:
            for c in range(RAW):
                raw_copy(c).wait_send()
                tilt_copy(c).wait_send()
            for o, f in peers:
                tot_copy(o, f, True).wait_send()
            hit_copy.wait_send()
        else:
            sent(s - 2)
    cross_wait(steps - 1)
    for u in range(n_subs):
        for direction in (0, 1):
            ring(u, steps - 1, direction)
    sent(steps - 3)

    part_copy.wait_recv()
    for u, (c0, w, part) in enumerate(subs):
        cols = pl.ds(c0, w)
        got = sums[rows_of((2 * steps - 1) * CHUNK + h * PART, PART), cols] + part_in[:, cols].astype(F32)
        for direction in (0, 1):
            for s in (steps - 2, steps - 1):
                ring_copy(direction, u, s, "half").wait_recv()
                got = got + recv[u][direction, s, pl.ds(0, PART)].astype(F32)
        out[:, cols] = got.astype(BF16)

    sent(steps - 2)
    sent(steps - 1)
    part_copy.wait_send()


def solution(mesh):
    nz, nv = mesh.shape["dp"] // 2, mesh.shape["vocab"]

    def shards(hidden, cotangent, token_ids, target_ids, loss_mask, embedding):
        tokens, width = hidden.shape
        rows = embedding.shape[0]
        half = tokens // 2
        steps = nz // 2
        shares = sum(share for share, _ in BLOCKS)
        subs, c0 = [], 0
        for share, early in BLOCKS:
            w = width // 128 * share // shares * 128
            subs.append((c0, w, EARLY if early else steps - 2))
            c0 += w
        any_space = pl.BlockSpec(memory_space=pl.ANY)
        dma = pltpu.SemaphoreType.DMA
        n = len(subs)
        scratch = [
            pltpu.VMEM((1, tokens), jnp.int32),
            pltpu.VMEM((2, 1, half), jnp.int32),
            pltpu.VMEM((2, 1, half), jnp.int32),
            pltpu.VMEM((2, half, width), BF16),
            pltpu.VMEM((tokens, width), BF16),
            pltpu.VMEM((rows, width), BF16),
            pltpu.VMEM((rows, half), BF16),
            pltpu.VMEM((rows, half), BF16),
            pltpu.VMEM((rows, half), F32),
            pltpu.VMEM((rows, half), BF16),
            pltpu.VMEM((rows, half), BF16),
            pltpu.VMEM((3, 1, half), F32),
            pltpu.VMEM((2 * nv, 1, half), F32),
            pltpu.VMEM((2, 1, half), F32),
            pltpu.VMEM((rows, width), F32),
            pltpu.VMEM((PART, width), BF16),
            pltpu.VMEM((PART, width), BF16),
            pltpu.VMEM((2, steps, PART, width), BF16),
            pltpu.VMEM((2, steps, PART, width), BF16),
        ]
        scratch += [pltpu.VMEM((2, steps, CHUNK, w), BF16) for _, w, _ in subs] * 2
        scratch += [
            dma((RAW + 6,)), dma((RAW,)), dma((RAW,)), dma((nv, 2)), dma((2 * nv,)),
            dma((RAW,)), dma((RAW,)), dma, dma,
            dma((2, n, steps)), dma((2, n, steps)), dma((2, n)), dma((2, n)),
            dma((2, steps)), dma((2, steps)), dma, dma,
        ]
        got = pl.pallas_call(
            functools.partial(kernel, nz, nv, subs),
            out_shape=jax.ShapeDtypeStruct((rows // (2 * nz), width), BF16),
            in_specs=[any_space] * 6,
            out_specs=pl.BlockSpec(memory_space=pltpu.VMEM),
            scratch_shapes=scratch,
            compiler_params=pltpu.CompilerParams(
                collective_id=0, has_side_effects=True, vmem_limit_bytes=VMEM_LIMIT
            ),
        )(
            hidden, cotangent, embedding,
            token_ids.reshape(1, tokens), target_ids.reshape(2, 1, half), loss_mask.reshape(2, 1, half),
        )
        return got[None]

    return jax.shard_map(
        shards,
        mesh=mesh,
        in_specs=(P("dp", "ends"), P("dp", "ends"), P("dp"), P("dp"), P("dp"), P("vocab", "ends")),
        out_specs=P("vocab", "dp", "ends"),
        check_vma=False,
    )
```

```python
import functools
import math

import jax
import jax.numpy as jnp
from jax import lax
from jax.experimental import pallas as pl
from jax.experimental.pallas import tpu as pltpu
from jax.sharding import PartitionSpec as P

D = 4608
SOFTCAP = 30.0
MESH = pl.DeviceIdType.MESH
F32 = jnp.float32
BF16 = jnp.bfloat16
VMEM_LIMIT = 62 * 2**20
PART = 16
CHUNK = 2 * PART
RAW = 4
EARLY = 2
BLOCKS = ((5, False), (4, False), (5, True), (4, True))


def dot_nt(a, b):
    return lax.dot_general(a, b, (((1,), (1,)), ((), ())), preferred_element_type=F32)


def dot_nn(a, b):
    return lax.dot_general(a, b, (((1,), (0,)), ((), ())), preferred_element_type=F32)


def rows_of(start, size):
    return pl.ds(pl.multiple_of(start, size), size)


def kernel(
    nz, nv, subs,
    hidden, cotangent, embedding, tokens_in, targets_in, mask_in,
    out,
    tokens, targets, mask, hid, cot, emb, raw_out, raw_in, own, tilt_out, tilt_in, stats, tot_in, hit_in, sums,
    part_out, part_in, cross_out, cross_in, *rest,
):
    n_subs = len(subs)
    send, recv, sems = rest[:n_subs], rest[n_subs : 2 * n_subs], rest[2 * n_subs :]
    (load, raw_s, raw_r, tot_s, tot_r, tilt_s, tilt_r, hit_s, hit_r, ring_s, ring_r, diag_s, diag_r,
     cross_s, cross_r, part_s, part_r) = sems

    d, v, e = lax.axis_index("dp"), lax.axis_index("vocab"), lax.axis_index("ends")
    z, h = d // 2, d % 2
    steps = nz // 2
    rows, half = own.shape
    width = hid.shape[2]

    def at_z(k, other):
        return (lax.rem(z + k + nz, nz) * 2 + (1 - h if other else h), v, e)

    mate = (d, v, 1 - e)
    across = (z * 2 + 1 - h, v, e)
    ahead = (1, -1)

    def peer(o, f):
        return (d, lax.rem(v + o, nv), (e + f) % 2)

    def chunk_at(place):
        s, direction = (place + 1) // 2, (place + 1) % 2
        return lax.rem(z + (steps - s if direction == 0 or place == 0 else steps + s), nz)

    def place_of(direction, s):
        return 0 if s == 0 else 2 * s - 1 + direction

    def ids_at(place, n):
        return lax.broadcasted_iota(jnp.int32, (CHUNK, n), 0) + (v * rows + chunk_at(place) * CHUNK)

    barrier = pltpu.get_barrier_semaphore()
    greet = [mate, across] + [at_z(k, o) for k in ahead for o in (False, True)] + [at_z(2 * k, False) for k in ahead]
    peers = [(o, f) for o in sorted(range(nv), key=lambda o: -min(o, nv - o)) for f in (1, 0) if (o, f) not in ((0, 0), (0, 1))]
    greet += [peer(o, f) for o, f in peers]
    peers.append((0, 1))
    for who in greet:
        pl.semaphore_signal(barrier, inc=1, device_id=who, device_id_type=MESH)

    quarter = rows // RAW
    per = quarter // CHUNK
    other_tokens, own_tokens = rows_of((1 - e) * half, half), rows_of(e * half, half)
    other_load = pltpu.make_async_copy(hidden.at[other_tokens], hid.at[1], load.at[0])
    other_load.start()
    for place in range(rows // CHUNK):
        pltpu.make_async_copy(
            embedding.at[rows_of(chunk_at(place) * CHUNK, CHUNK)], emb.at[pl.ds(place * CHUNK, CHUNK)],
            load.at[1 + place // per],
        ).start()
    pairs = [(hidden.at[own_tokens], hid.at[0]), (targets_in, targets), (mask_in, mask), (tokens_in, tokens), (cotangent, cot)]
    loads = [pltpu.make_async_copy(a, b, load.at[1 + RAW + i]) for i, (a, b) in enumerate(pairs)]

    def raw_copy(c):
        block = pl.ds(c * quarter, quarter)
        return pltpu.make_async_remote_copy(
            src_ref=raw_out.at[block], dst_ref=raw_in.at[block], send_sem=raw_s.at[c], recv_sem=raw_r.at[c],
            device_id=mate, device_id_type=MESH,
        )

    other_load.wait()
    for c in range(RAW):
        block = pl.ds(c * quarter, quarter)
        pltpu.make_async_copy(embedding.at[block], emb.at[block], load.at[1 + c]).wait()
        raw_out[block] = dot_nt(emb[block], hid[1]).astype(BF16)
        if c == 0:
            pl.semaphore_wait(barrier, len(greet))
        raw_copy(c).start()

    for copy in loads:
        copy.start()
    loads[0].wait()
    for c in range(RAW):
        block = pl.ds(c * quarter, quarter)
        own[block] = dot_nt(emb[block], hid[0])
    loads[1].wait()
    loads[2].wait()

    def tilt_copy(c):
        block = pl.ds(c * quarter, quarter)
        return pltpu.make_async_remote_copy(
            src_ref=tilt_out.at[block], dst_ref=tilt_in.at[block], send_sem=tilt_s.at[c], recv_sem=tilt_r.at[c],
            device_id=mate, device_id_type=MESH,
        )

    def summed(x):
        return jnp.sum(x, axis=0, keepdims=True)

    nothing = jnp.zeros((1, half), F32)
    total, at_shifted, at_slope = nothing, nothing, nothing
    for c in range(RAW):
        raw_copy(c).wait_recv()
        for place in range(c * per, (c + 1) * per):
            block = pl.ds(place * CHUNK, CHUNK)
            t = jnp.tanh((own[block] + raw_in[block].astype(F32)) * (1.0 / SOFTCAP))
            s = jnp.exp(t * SOFTCAP - SOFTCAP)
            slope = 1.0 - t * t
            tilt = s * slope
            own[block] = tilt
            tilt_out[block] = tilt.astype(BF16)
            hit = targets[e] == ids_at(place, half)
            total = total + summed(s)
            at_shifted = at_shifted + summed(jnp.where(hit, s, 0.0))
            at_slope = at_slope + summed(jnp.where(hit, slope, 0.0))
        tilt_copy(c).start()
    stats[0], stats[1], stats[2] = total, at_shifted, at_slope

    def tot_copy(o, f, sent):
        source = (lax.rem(v + o, nv) * 2 + (e + f) % 2) if not sent else v * 2 + e
        return pltpu.make_async_remote_copy(
            src_ref=stats.at[0], dst_ref=tot_in.at[source], send_sem=tot_s.at[o, f], recv_sem=tot_r.at[source],
            device_id=peer(o, f), device_id_type=MESH,
        )

    hit_copy = pltpu.make_async_remote_copy(
        src_ref=stats.at[pl.ds(1, 2)], dst_ref=hit_in, send_sem=hit_s, recv_sem=hit_r, device_id=mate, device_id_type=MESH,
    )
    for o, f in peers:
        tot_copy(o, f, True).start()
    hit_copy.start()
    loads[3].wait()
    loads[4].wait()
    normalizer = jnp.asarray(math.sqrt(D), F32).astype(BF16).astype(F32)
    for c in range(RAW):
        block = pl.ds(c * quarter, quarter)
        picks = [jnp.where(tokens[...] == ids_at(c * per + i, 2 * half), normalizer, 0.0).astype(BF16) for i in range(per)]
        picks = jnp.concatenate(picks, axis=0)
        for c0, w, _ in subs:
            sums[block, pl.ds(c0, w)] = dot_nn(picks, cot[:, pl.ds(c0, w)])

    totals = [total, nothing]
    for o, f in peers:
        tot_copy(o, f, False).wait_recv()
        totals[f] = totals[f] + tot_in[lax.rem(v + o, nv) * 2 + (e + f) % 2]
    hit_copy.wait_recv()
    factors, at_target, wanted = [], [], []
    for f, (a, b) in enumerate(((at_shifted, at_slope), (hit_in[0], hit_in[1]))):
        side = (e + f) % 2
        weight = mask[side].astype(F32)
        inverse = 1.0 / totals[f]
        factors.append(weight * inverse)
        at_target.append(weight * (a * inverse - 1.0) * b)
        wanted.append(targets[side])

    come = []

    def complete(places):
        for c in sorted({place // per for place in places}):
            if c not in come:
                tilt_copy(c).wait_recv()
                come.append(c)
        blocks = [pl.ds(place * CHUNK, CHUNK) for place in places]
        left = []
        for f, tilts in enumerate((own, tilt_in)):
            parts = []
            for place, b in zip(places, blocks):
                hit = wanted[f] == ids_at(place, half)
                parts.append(jnp.where(hit, at_target[f], factors[f] * tilts[b].astype(F32)).astype(BF16))
            left.append(parts[0] if len(parts) == 1 else jnp.concatenate(parts, axis=0))
        for c0, w, _ in subs:
            cols = pl.ds(c0, w)
            got = dot_nn(left[0], hid[0, :, cols]) + dot_nn(left[1], hid[1, :, cols])
            for i, b in enumerate(blocks):
                sums[b, cols] = sums[b, cols] + got[i * CHUNK : (i + 1) * CHUNK]

    straight_rows, other_rows = rows_of(h * PART, PART), rows_of((1 - h) * PART, PART)

    def ring_copy(direction, u, s, kind):
        source, landing = {
            "full": (pl.ds(0, CHUNK), pl.ds(0, CHUNK)),
            "part": (straight_rows, pl.ds(0, PART)),
            "half": (pl.ds(0, PART), pl.ds(0, PART)),
        }[kind]
        return pltpu.make_async_remote_copy(
            src_ref=send[u].at[direction, s, source], dst_ref=recv[u].at[direction, s, landing],
            send_sem=ring_s.at[direction, u, s], recv_sem=ring_r.at[direction, u, s],
            device_id=at_z(ahead[direction] * (2 if s == steps - 2 else 1), False), device_id_type=MESH,
        )

    def diag_copy(direction, u):
        s = subs[u][2] - 1
        return pltpu.make_async_remote_copy(
            src_ref=send[u].at[direction, s, other_rows], dst_ref=recv[u].at[direction, s, pl.ds(PART, PART)],
            send_sem=diag_s.at[direction, u], recv_sem=diag_r.at[direction, u],
            device_id=at_z(ahead[direction], True), device_id_type=MESH,
        )

    def cross_cols(s):
        c0 = min(lo for lo, _, part in subs if part <= s)
        return pl.ds(c0, width - c0)

    def cross_copy(direction, s):
        cols = cross_cols(s)
        return pltpu.make_async_remote_copy(
            src_ref=cross_out.at[direction, s, :, cols], dst_ref=cross_in.at[direction, s, :, cols],
            send_sem=cross_s.at[direction, s], recv_sem=cross_r.at[direction, s],
            device_id=across, device_id_type=MESH,
        )

    part_copy = pltpu.make_async_remote_copy(
        src_ref=part_out, dst_ref=part_in, send_sem=part_s, recv_sem=part_r, device_id=across, device_id_type=MESH,
    )
    def row_start(direction, s):
        return place_of(direction, s) * CHUNK

    def cross_start(s):
        cols = cross_cols(s)
        for direction in (0, 1):
            block = rows_of(row_start(direction, s) + (1 - h) * PART, PART)
            cross_out[direction, s, :, cols] = sums[block, cols].astype(BF16)
            cross_copy(direction, s).start()

    def begin(u, direction):
        return 0 if direction == u % 2 else 1

    def ring(u, s, direction):
        c0, w, part = subs[u]
        cols = pl.ds(c0, w)
        start = row_start(direction, s)
        if s >= part:
            got = sums[rows_of(start + h * PART, PART), cols] + cross_in[direction, s, :, cols].astype(F32)
            if begin(u, direction) < s < steps - 1:
                ring_copy(direction, u, s - 1, "part" if s == part else "half").wait_recv()
                got = got + recv[u][direction, s - 1, pl.ds(0, PART)].astype(F32)
                if s == part:
                    diag_copy(direction, u).wait_recv()
                    got = got + recv[u][direction, s - 1, pl.ds(PART, PART)].astype(F32)
            send[u][direction, s, pl.ds(0, PART)] = got.astype(BF16)
            ring_copy(direction, u, s, "half").start()
            return
        got = sums[pl.ds(start, CHUNK), cols]
        if s > begin(u, direction):
            ring_copy(direction, u, s - 1, "full").wait_recv()
            got = got + recv[u][direction, s - 1].astype(F32)
        send[u][direction, s] = got.astype(BF16)
        if s == part - 1:
            diag_copy(direction, u).start()
            ring_copy(direction, u, s, "part").start()
        else:
            ring_copy(direction, u, s, "full").start()

    def pair(s):
        return [place_of(0, s), place_of(1, s)]

    def cross_wait(s):
        for direction in (0, 1):
            cross_copy(direction, s).wait_recv()

    def sent(s):
        for direction in (0, 1):
            if s >= EARLY:
                cross_copy(direction, s).wait_send()
            for u, (_, _, part) in enumerate(subs):
                if s >= begin(u, direction):
                    kind = "full" if s < part - 1 else "part" if s == part - 1 else "half"
                    ring_copy(direction, u, s, kind).wait_send()
                    if kind == "part":
                        diag_copy(direction, u).wait_send()

    complete([0])
    for u in range(n_subs):
        ring(u, 0, u % 2)
    complete(pair(1))
    if EARLY == 1:
        cross_start(1)
    for u, (_, _, part) in enumerate(subs):
        if part > 1:
            ring(u, 1, 1 - u % 2)
    for s in (2, 3):
        complete(pair(s))
        if s >= EARLY:
            cross_start(s)
    if EARLY == 1:
        cross_wait(1)
        for u, (_, _, part) in enumerate(subs):
            if part == 1:
                ring(u, 1, 1 - u % 2)
    for s in range(1, steps - 1):
        if s >= EARLY:
            cross_wait(s)
        for u in range(n_subs):
            for direction in (0, 1):
                if s > begin(u, direction):
                    ring(u, s, direction)
        if s < steps - 3:
            complete(pair(s + 3))
            if s + 3 >= EARLY:
                cross_start(s + 3)
        if s == steps - 3:
            cross_wait(steps - 1)
            for u in range(n_subs):
                for direction in (0, 1):
                    ring(u, steps - 1, direction)
            complete([2 * steps - 1])
            part_out[...] = sums[rows_of((2 * steps - 1) * CHUNK + (1 - h) * PART, PART)].astype(BF16)
            part_copy.start()
        if s == 1:
            for c in range(RAW):
                raw_copy(c).wait_send()
                tilt_copy(c).wait_send()
            for o, f in peers:
                tot_copy(o, f, True).wait_send()
            hit_copy.wait_send()
        else:
            sent(s - 2)
    sent(steps - 3)

    part_copy.wait_recv()
    for u, (c0, w, part) in enumerate(subs):
        cols = pl.ds(c0, w)
        got = sums[rows_of((2 * steps - 1) * CHUNK + h * PART, PART), cols] + part_in[:, cols].astype(F32)
        for direction in (0, 1):
            for s in (steps - 2, steps - 1):
                ring_copy(direction, u, s, "half").wait_recv()
                got = got + recv[u][direction, s, pl.ds(0, PART)].astype(F32)
        out[:, cols] = got.astype(BF16)

    sent(steps - 2)
    sent(steps - 1)
    part_copy.wait_send()


def solution(mesh):
    nz, nv = mesh.shape["dp"] // 2, mesh.shape["vocab"]

    def shards(hidden, cotangent, token_ids, target_ids, loss_mask, embedding):
        tokens, width = hidden.shape
        rows = embedding.shape[0]
        half = tokens // 2
        steps = nz // 2
        shares = sum(share for share, _ in BLOCKS)
        subs, c0 = [], 0
        for share, early in BLOCKS:
            w = width // 128 * share // shares * 128
            subs.append((c0, w, EARLY if early else steps - 2))
            c0 += w
        any_space = pl.BlockSpec(memory_space=pl.ANY)
        dma = pltpu.SemaphoreType.DMA
        n = len(subs)
        scratch = [
            pltpu.VMEM((1, tokens), jnp.int32),
            pltpu.VMEM((2, 1, half), jnp.int32),
            pltpu.VMEM((2, 1, half), jnp.int32),
            pltpu.VMEM((2, half, width), BF16),
            pltpu.VMEM((tokens, width), BF16),
            pltpu.VMEM((rows, width), BF16),
            pltpu.VMEM((rows, half), BF16),
            pltpu.VMEM((rows, half), BF16),
            pltpu.VMEM((rows, half), F32),
            pltpu.VMEM((rows, half), BF16),
            pltpu.VMEM((rows, half), BF16),
            pltpu.VMEM((3, 1, half), F32),
            pltpu.VMEM((2 * nv, 1, half), F32),
            pltpu.VMEM((2, 1, half), F32),
            pltpu.VMEM((rows, width), F32),
            pltpu.VMEM((PART, width), BF16),
            pltpu.VMEM((PART, width), BF16),
            pltpu.VMEM((2, steps, PART, width), BF16),
            pltpu.VMEM((2, steps, PART, width), BF16),
        ]
        scratch += [pltpu.VMEM((2, steps, CHUNK, w), BF16) for _, w, _ in subs] * 2
        scratch += [
            dma((RAW + 6,)), dma((RAW,)), dma((RAW,)), dma((nv, 2)), dma((2 * nv,)),
            dma((RAW,)), dma((RAW,)), dma, dma,
            dma((2, n, steps)), dma((2, n, steps)), dma((2, n)), dma((2, n)),
            dma((2, steps)), dma((2, steps)), dma, dma,
        ]
        got = pl.pallas_call(
            functools.partial(kernel, nz, nv, subs),
            out_shape=jax.ShapeDtypeStruct((rows // (2 * nz), width), BF16),
            in_specs=[any_space] * 6,
            out_specs=pl.BlockSpec(memory_space=pltpu.VMEM),
            scratch_shapes=scratch,
            compiler_params=pltpu.CompilerParams(
                collective_id=0, has_side_effects=True, vmem_limit_bytes=VMEM_LIMIT
            ),
        )(
            hidden, cotangent, embedding,
            token_ids.reshape(1, tokens), target_ids.reshape(2, 1, half), loss_mask.reshape(2, 1, half),
        )
        return got[None]

    return jax.shard_map(
        shards,
        mesh=mesh,
        in_specs=(P("dp", "ends"), P("dp", "ends"), P("dp"), P("dp"), P("dp"), P("vocab", "ends")),
        out_specs=P("vocab", "dp", "ends"),
        check_vma=False,
    )
```

```python
import functools
import math

import jax
import jax.numpy as jnp
from jax import lax
from jax.experimental import pallas as pl
from jax.experimental.pallas import tpu as pltpu
from jax.sharding import PartitionSpec as P

D = 4608
SOFTCAP = 30.0
MESH = pl.DeviceIdType.MESH
F32 = jnp.float32
BF16 = jnp.bfloat16
VMEM_LIMIT = 62 * 2**20
PART = 16
CHUNK = 2 * PART
RAW = 4
EARLY = 2
BLOCKS = ((5, False), (4, False), (5, True), (4, True))


def dot_nt(a, b):
    return lax.dot_general(a, b, (((1,), (1,)), ((), ())), preferred_element_type=F32)


def dot_nn(a, b):
    return lax.dot_general(a, b, (((1,), (0,)), ((), ())), preferred_element_type=F32)


def rows_of(start, size):
    return pl.ds(pl.multiple_of(start, size), size)


def kernel(
    nz, nv, subs,
    hidden, cotangent, embedding, tokens_in, targets_in, mask_in,
    out,
    tokens, targets, mask, hid, cot, emb, raw_out, raw_in, own, tilt_out, tilt_in, stats, tot_in, hit_in, sums,
    part_out, part_in, cross_out, cross_in, *rest,
):
    n_subs = len(subs)
    send, recv, sems = rest[:n_subs], rest[n_subs : 2 * n_subs], rest[2 * n_subs :]
    (load, raw_s, raw_r, tot_s, tot_r, tilt_s, tilt_r, hit_s, hit_r, ring_s, ring_r, diag_s, diag_r,
     cross_s, cross_r, part_s, part_r) = sems

    d, v, e = lax.axis_index("dp"), lax.axis_index("vocab"), lax.axis_index("ends")
    z, h = d // 2, d % 2
    steps = nz // 2
    rows, half = own.shape
    width = hid.shape[2]

    def at_z(k, other):
        return (lax.rem(z + k + nz, nz) * 2 + (1 - h if other else h), v, e)

    mate = (d, v, 1 - e)
    across = (z * 2 + 1 - h, v, e)
    ahead = (1, -1)

    def peer(o, f):
        return (d, lax.rem(v + o, nv), (e + f) % 2)

    def chunk_at(place):
        s, direction = (place + 1) // 2, (place + 1) % 2
        return lax.rem(z + (steps - s if direction == 0 or place == 0 else steps + s), nz)

    def place_of(direction, s):
        return 0 if s == 0 else 2 * s - 1 + direction

    def ids_at(place, n):
        return lax.broadcasted_iota(jnp.int32, (CHUNK, n), 0) + (v * rows + chunk_at(place) * CHUNK)

    barrier = pltpu.get_barrier_semaphore()
    greet = [mate, across] + [at_z(k, o) for k in ahead for o in (False, True)] + [at_z(2 * k, False) for k in ahead]
    peers = [(o, f) for o in sorted(range(nv), key=lambda o: -min(o, nv - o)) for f in (1, 0) if (o, f) not in ((0, 0), (0, 1))]
    greet += [peer(o, f) for o, f in peers]
    peers.append((0, 1))
    for who in greet:
        pl.semaphore_signal(barrier, inc=1, device_id=who, device_id_type=MESH)

    quarter = rows // RAW
    per = quarter // CHUNK
    other_tokens, own_tokens = rows_of((1 - e) * half, half), rows_of(e * half, half)
    other_load = pltpu.make_async_copy(hidden.at[other_tokens], hid.at[1], load.at[0])
    other_load.start()
    for place in range(rows // CHUNK):
        pltpu.make_async_copy(
            embedding.at[rows_of(chunk_at(place) * CHUNK, CHUNK)], emb.at[pl.ds(place * CHUNK, CHUNK)],
            load.at[1 + place // per],
        ).start()
    pairs = [(hidden.at[own_tokens], hid.at[0]), (targets_in, targets), (mask_in, mask), (tokens_in, tokens), (cotangent, cot)]
    loads = [pltpu.make_async_copy(a, b, load.at[1 + RAW + i]) for i, (a, b) in enumerate(pairs)]

    def raw_copy(c):
        block = pl.ds(c * quarter, quarter)
        return pltpu.make_async_remote_copy(
            src_ref=raw_out.at[block], dst_ref=raw_in.at[block], send_sem=raw_s.at[c], recv_sem=raw_r.at[c],
            device_id=mate, device_id_type=MESH,
        )

    other_load.wait()
    for c in range(RAW):
        block = pl.ds(c * quarter, quarter)
        pltpu.make_async_copy(embedding.at[block], emb.at[block], load.at[1 + c]).wait()
        raw_out[block] = dot_nt(emb[block], hid[1]).astype(BF16)
        if c == 0:
            pl.semaphore_wait(barrier, len(greet))
        raw_copy(c).start()

    for copy in loads:
        copy.start()
    loads[0].wait()
    for c in range(RAW):
        block = pl.ds(c * quarter, quarter)
        own[block] = dot_nt(emb[block], hid[0])
    loads[1].wait()
    loads[2].wait()

    def tilt_copy(c):
        block = pl.ds(c * quarter, quarter)
        return pltpu.make_async_remote_copy(
            src_ref=tilt_out.at[block], dst_ref=tilt_in.at[block], send_sem=tilt_s.at[c], recv_sem=tilt_r.at[c],
            device_id=mate, device_id_type=MESH,
        )

    def summed(x):
        return jnp.sum(x, axis=0, keepdims=True)

    nothing = jnp.zeros((1, half), F32)
    total, at_shifted, at_slope = nothing, nothing, nothing
    for c in range(RAW):
        raw_copy(c).wait_recv()
        for place in range(c * per, (c + 1) * per):
            block = pl.ds(place * CHUNK, CHUNK)
            t = jnp.tanh((own[block] + raw_in[block].astype(F32)) * (1.0 / SOFTCAP))
            s = jnp.exp(t * SOFTCAP - SOFTCAP)
            slope = 1.0 - t * t
            tilt = s * slope
            own[block] = tilt
            tilt_out[block] = tilt.astype(BF16)
            hit = targets[e] == ids_at(place, half)
            total = total + summed(s)
            at_shifted = at_shifted + summed(jnp.where(hit, s, 0.0))
            at_slope = at_slope + summed(jnp.where(hit, slope, 0.0))
        if c < RAW - 1:
            tilt_copy(c).start()
    stats[0], stats[1], stats[2] = total, at_shifted, at_slope

    def tot_copy(o, f, sent):
        source = (lax.rem(v + o, nv) * 2 + (e + f) % 2) if not sent else v * 2 + e
        return pltpu.make_async_remote_copy(
            src_ref=stats.at[0], dst_ref=tot_in.at[source], send_sem=tot_s.at[o, f], recv_sem=tot_r.at[source],
            device_id=peer(o, f), device_id_type=MESH,
        )

    hit_copy = pltpu.make_async_remote_copy(
        src_ref=stats.at[pl.ds(1, 2)], dst_ref=hit_in, send_sem=hit_s, recv_sem=hit_r, device_id=mate, device_id_type=MESH,
    )
    for o, f in peers:
        tot_copy(o, f, True).start()
    hit_copy.start()
    tilt_copy(RAW - 1).start()
    loads[3].wait()
    loads[4].wait()
    normalizer = jnp.asarray(math.sqrt(D), F32).astype(BF16).astype(F32)
    for c in range(RAW):
        block = pl.ds(c * quarter, quarter)
        picks = [jnp.where(tokens[...] == ids_at(c * per + i, 2 * half), normalizer, 0.0).astype(BF16) for i in range(per)]
        picks = jnp.concatenate(picks, axis=0)
        for c0, w, _ in subs:
            sums[block, pl.ds(c0, w)] = dot_nn(picks, cot[:, pl.ds(c0, w)])

    totals = [total, nothing]
    for o, f in peers:
        tot_copy(o, f, False).wait_recv()
        totals[f] = totals[f] + tot_in[lax.rem(v + o, nv) * 2 + (e + f) % 2]
    hit_copy.wait_recv()
    factors, at_target, wanted = [], [], []
    for f, (a, b) in enumerate(((at_shifted, at_slope), (hit_in[0], hit_in[1]))):
        side = (e + f) % 2
        weight = mask[side].astype(F32)
        inverse = 1.0 / totals[f]
        factors.append(weight * inverse)
        at_target.append(weight * (a * inverse - 1.0) * b)
        wanted.append(targets[side])

    come = []

    def complete(places):
        for c in sorted({place // per for place in places}):
            if c not in come:
                tilt_copy(c).wait_recv()
                come.append(c)
        blocks = [pl.ds(place * CHUNK, CHUNK) for place in places]
        left = []
        for f, tilts in enumerate((own, tilt_in)):
            parts = []
            for place, b in zip(places, blocks):
                hit = wanted[f] == ids_at(place, half)
                parts.append(jnp.where(hit, at_target[f], factors[f] * tilts[b].astype(F32)).astype(BF16))
            left.append(parts[0] if len(parts) == 1 else jnp.concatenate(parts, axis=0))
        for c0, w, _ in subs:
            cols = pl.ds(c0, w)
            got = dot_nn(left[0], hid[0, :, cols]) + dot_nn(left[1], hid[1, :, cols])
            for i, b in enumerate(blocks):
                sums[b, cols] = sums[b, cols] + got[i * CHUNK : (i + 1) * CHUNK]

    straight_rows, other_rows = rows_of(h * PART, PART), rows_of((1 - h) * PART, PART)

    def ring_copy(direction, u, s, kind):
        source, landing = {
            "full": (pl.ds(0, CHUNK), pl.ds(0, CHUNK)),
            "part": (straight_rows, pl.ds(0, PART)),
            "half": (pl.ds(0, PART), pl.ds(0, PART)),
        }[kind]
        return pltpu.make_async_remote_copy(
            src_ref=send[u].at[direction, s, source], dst_ref=recv[u].at[direction, s, landing],
            send_sem=ring_s.at[direction, u, s], recv_sem=ring_r.at[direction, u, s],
            device_id=at_z(ahead[direction] * (2 if s == steps - 2 else 1), False), device_id_type=MESH,
        )

    def diag_copy(direction, u):
        s = subs[u][2] - 1
        return pltpu.make_async_remote_copy(
            src_ref=send[u].at[direction, s, other_rows], dst_ref=recv[u].at[direction, s, pl.ds(PART, PART)],
            send_sem=diag_s.at[direction, u], recv_sem=diag_r.at[direction, u],
            device_id=at_z(ahead[direction], True), device_id_type=MESH,
        )

    def cross_cols(s):
        c0 = min(lo for lo, _, part in subs if part <= s)
        return pl.ds(c0, width - c0)

    def cross_copy(direction, s):
        cols = cross_cols(s)
        return pltpu.make_async_remote_copy(
            src_ref=cross_out.at[direction, s, :, cols], dst_ref=cross_in.at[direction, s, :, cols],
            send_sem=cross_s.at[direction, s], recv_sem=cross_r.at[direction, s],
            device_id=across, device_id_type=MESH,
        )

    part_copy = pltpu.make_async_remote_copy(
        src_ref=part_out, dst_ref=part_in, send_sem=part_s, recv_sem=part_r, device_id=across, device_id_type=MESH,
    )
    def row_start(direction, s):
        return place_of(direction, s) * CHUNK

    def cross_start(s):
        cols = cross_cols(s)
        for direction in (0, 1):
            block = rows_of(row_start(direction, s) + (1 - h) * PART, PART)
            cross_out[direction, s, :, cols] = sums[block, cols].astype(BF16)
            cross_copy(direction, s).start()

    def begin(u, direction):
        return 0 if direction == u % 2 else 1

    def ring(u, s, direction):
        c0, w, part = subs[u]
        cols = pl.ds(c0, w)
        start = row_start(direction, s)
        if s >= part:
            got = sums[rows_of(start + h * PART, PART), cols] + cross_in[direction, s, :, cols].astype(F32)
            if begin(u, direction) < s < steps - 1:
                ring_copy(direction, u, s - 1, "part" if s == part else "half").wait_recv()
                got = got + recv[u][direction, s - 1, pl.ds(0, PART)].astype(F32)
                if s == part:
                    diag_copy(direction, u).wait_recv()
                    got = got + recv[u][direction, s - 1, pl.ds(PART, PART)].astype(F32)
            send[u][direction, s, pl.ds(0, PART)] = got.astype(BF16)
            ring_copy(direction, u, s, "half").start()
            return
        got = sums[pl.ds(start, CHUNK), cols]
        if s > begin(u, direction):
            ring_copy(direction, u, s - 1, "full").wait_recv()
            got = got + recv[u][direction, s - 1].astype(F32)
        send[u][direction, s] = got.astype(BF16)
        if s == part - 1:
            diag_copy(direction, u).start()
            ring_copy(direction, u, s, "part").start()
        else:
            ring_copy(direction, u, s, "full").start()

    def pair(s):
        return [place_of(0, s), place_of(1, s)]

    def cross_wait(s):
        for direction in (0, 1):
            cross_copy(direction, s).wait_recv()

    def sent(s):
        for direction in (0, 1):
            if s >= EARLY:
                cross_copy(direction, s).wait_send()
            for u, (_, _, part) in enumerate(subs):
                if s >= begin(u, direction):
                    kind = "full" if s < part - 1 else "part" if s == part - 1 else "half"
                    ring_copy(direction, u, s, kind).wait_send()
                    if kind == "part":
                        diag_copy(direction, u).wait_send()

    complete([0])
    for u in range(n_subs):
        ring(u, 0, u % 2)
    complete(pair(1))
    if EARLY == 1:
        cross_start(1)
    for u, (_, _, part) in enumerate(subs):
        if part > 1:
            ring(u, 1, 1 - u % 2)
    for s in (2, 3):
        complete(pair(s))
        if s >= EARLY:
            cross_start(s)
    if EARLY == 1:
        cross_wait(1)
        for u, (_, _, part) in enumerate(subs):
            if part == 1:
                ring(u, 1, 1 - u % 2)
    for s in range(1, steps - 1):
        if s >= EARLY:
            cross_wait(s)
        for u in range(n_subs):
            for direction in (0, 1):
                if s > begin(u, direction):
                    ring(u, s, direction)
        if s < steps - 3:
            complete(pair(s + 3))
            if s + 3 >= EARLY:
                cross_start(s + 3)
        if s == steps - 3:
            cross_wait(steps - 1)
            for u in range(n_subs):
                for direction in (0, 1):
                    ring(u, steps - 1, direction)
            complete([2 * steps - 1])
            part_out[...] = sums[rows_of((2 * steps - 1) * CHUNK + (1 - h) * PART, PART)].astype(BF16)
            part_copy.start()
        if s == 1:
            for c in range(RAW):
                raw_copy(c).wait_send()
                tilt_copy(c).wait_send()
            for o, f in peers:
                tot_copy(o, f, True).wait_send()
            hit_copy.wait_send()
        else:
            sent(s - 2)
    sent(steps - 3)

    part_copy.wait_recv()
    for u, (c0, w, part) in enumerate(subs):
        cols = pl.ds(c0, w)
        got = sums[rows_of((2 * steps - 1) * CHUNK + h * PART, PART), cols] + part_in[:, cols].astype(F32)
        for direction in (0, 1):
            for s in (steps - 2, steps - 1):
                ring_copy(direction, u, s, "half").wait_recv()
                got = got + recv[u][direction, s, pl.ds(0, PART)].astype(F32)
        out[:, cols] = got.astype(BF16)

    sent(steps - 2)
    sent(steps - 1)
    part_copy.wait_send()


def solution(mesh):
    nz, nv = mesh.shape["dp"] // 2, mesh.shape["vocab"]

    def shards(hidden, cotangent, token_ids, target_ids, loss_mask, embedding):
        tokens, width = hidden.shape
        rows = embedding.shape[0]
        half = tokens // 2
        steps = nz // 2
        shares = sum(share for share, _ in BLOCKS)
        subs, c0 = [], 0
        for share, early in BLOCKS:
            w = width // 128 * share // shares * 128
            subs.append((c0, w, EARLY if early else steps - 2))
            c0 += w
        any_space = pl.BlockSpec(memory_space=pl.ANY)
        dma = pltpu.SemaphoreType.DMA
        n = len(subs)
        scratch = [
            pltpu.VMEM((1, tokens), jnp.int32),
            pltpu.VMEM((2, 1, half), jnp.int32),
            pltpu.VMEM((2, 1, half), jnp.int32),
            pltpu.VMEM((2, half, width), BF16),
            pltpu.VMEM((tokens, width), BF16),
            pltpu.VMEM((rows, width), BF16),
            pltpu.VMEM((rows, half), BF16),
            pltpu.VMEM((rows, half), BF16),
            pltpu.VMEM((rows, half), F32),
            pltpu.VMEM((rows, half), BF16),
            pltpu.VMEM((rows, half), BF16),
            pltpu.VMEM((3, 1, half), F32),
            pltpu.VMEM((2 * nv, 1, half), F32),
            pltpu.VMEM((2, 1, half), F32),
            pltpu.VMEM((rows, width), F32),
            pltpu.VMEM((PART, width), BF16),
            pltpu.VMEM((PART, width), BF16),
            pltpu.VMEM((2, steps, PART, width), BF16),
            pltpu.VMEM((2, steps, PART, width), BF16),
        ]
        scratch += [pltpu.VMEM((2, steps, CHUNK, w), BF16) for _, w, _ in subs] * 2
        scratch += [
            dma((RAW + 6,)), dma((RAW,)), dma((RAW,)), dma((nv, 2)), dma((2 * nv,)),
            dma((RAW,)), dma((RAW,)), dma, dma,
            dma((2, n, steps)), dma((2, n, steps)), dma((2, n)), dma((2, n)),
            dma((2, steps)), dma((2, steps)), dma, dma,
        ]
        got = pl.pallas_call(
            functools.partial(kernel, nz, nv, subs),
            out_shape=jax.ShapeDtypeStruct((rows // (2 * nz), width), BF16),
            in_specs=[any_space] * 6,
            out_specs=pl.BlockSpec(memory_space=pltpu.VMEM),
            scratch_shapes=scratch,
            compiler_params=pltpu.CompilerParams(
                collective_id=0, has_side_effects=True, vmem_limit_bytes=VMEM_LIMIT
            ),
        )(
            hidden, cotangent, embedding,
            token_ids.reshape(1, tokens), target_ids.reshape(2, 1, half), loss_mask.reshape(2, 1, half),
        )
        return got[None]

    return jax.shard_map(
        shards,
        mesh=mesh,
        in_specs=(P("dp", "ends"), P("dp", "ends"), P("dp"), P("dp"), P("dp"), P("vocab", "ends")),
        out_specs=P("vocab", "dp", "ends"),
        check_vma=False,
    )
```
